32 devices in a mesh: parts: 2 (over y), seq: 4 (over z), layer: 4 (over x, core).
Axes of the slice: x: 2, y: 2, z: 4, core: 2. Of those that a mesh axis runs over, the one named last changes fastest.
Arguments:
- store: bfloat16 [2048, 16384], P(('parts', 'seq'), 'layer'), parts along dimension 0, may hold values from -0.046875 to 0.046875
- queries: float32 [256, 16384], P('seq', 'layer'), may hold values from -6 to 6
- owner: int32 [8], replicated, may hold values from 0 to 7, each once
- eig_in: float32 [8, 32, 32], replicated, may hold values from -1 to 1
- eig_out: float32 [8, 64, 64], replicated, may hold values from -0.75 to 0.75
- eig_val: float32 [8, 32, 64], replicated, may hold values from 0.05 to 1
- query_order: int32 [256], replicated, may hold values from 0 to 255, each once
Outputs:
- scores: float32 [2048, 256], P(('parts', 'seq', 'layer')), parts along dimension 0
The draws below stay inside these ranges and needn't reach their ends.
There are 2 independent parts, one for each index of `parts`. The reference program is written for one: setup_inputs(seed, part) draws one part's arguments, and reference() takes and returns one part's arrays. A program takes and returns all parts, laid end to end along the dimension named above; an argument that names none is the same for every part. Nothing has to cross between parts.
Inputs may be any that keep to these rules, and one draw needn't show every extreme that they name: `owner`: each layer appears once. `query_order`: each query appears once.
All inputs are finite; a program needn't handle non-finite values.
Results may differ from the reference program's by a relative error of at most 0.0029.
Values may be sent and summed in bfloat16 or wider, within the bound.
A program may use at most 64 MiB of HBM per device.

```python
import math
import jax
import jax.numpy as jnp
from jax import lax

A = 32
B = 64
NQ = 256
LAYERS = 8
NSEQ = 1024


def levels(key, dims, shards, smallest, top_value):
    factor_of, own = 1.0, jax.random.fold_in(key, 6)
    for dim, parts in shards:
        steps = jnp.exp(jax.random.uniform(jax.random.fold_in(own, dim), (parts,), jnp.float32, smallest / len(shards), top_value / len(shards)))
        factor_of = factor_of * jnp.repeat(steps, dims[dim] // parts).reshape([-1 if axis == dim else 1 for axis in range(len(dims))])
    return factor_of


def bell_draw(key, dims, spread, most, pieces=(), held_as=jnp.bfloat16):
    level = levels(key, dims, pieces, -0.22, 0.18) if pieces else 1.0
    array = jax.random.normal(key, dims, jnp.float32) * spread * level
    return jnp.minimum(jnp.maximum(array, -most), most).astype(held_as)


def setup_inputs(seed: int = 0, part: int = 0) -> dict:
    key_of = jax.random.split(jax.random.key(seed), 8)
    own_keys = jax.random.split(jax.random.fold_in(key_of[7], part), 8)
    store = bell_draw(own_keys[0], (NSEQ, LAYERS * A * B), (LAYERS * A * B) ** -0.5, 0.046875, ((0, 4), (1, 4)))
    queries = bell_draw(key_of[1], (NQ, LAYERS * A * B), 1.0, 6.0, ((0, 4), (1, 4)), jnp.float32)
    owner = jax.random.permutation(key_of[2], LAYERS).astype(jnp.int32)
    eig_in = bell_draw(key_of[3], (LAYERS, A, A), A ** -0.5, 1.0, (), jnp.float32)
    eig_out = bell_draw(key_of[4], (LAYERS, B, B), B ** -0.5, 0.75, (), jnp.float32)
    eig_val = jnp.clip(jnp.exp(jax.random.uniform(key_of[5], (LAYERS, A, B), jnp.float32, math.log(0.05), math.log(1.0))), 0.05, 1.0)
    query_order = jax.random.permutation(key_of[6], NQ).astype(jnp.int32)
    return dict(store=store, queries=queries, owner=owner, eig_in=eig_in, eig_out=eig_out, eig_val=eig_val, query_order=query_order)


def precondition(grads, basis_in, basis_out, values):
    rotated = jnp.einsum('tai,qtab,tbj->qtij', basis_in, grads, basis_out, precision=lax.Precision.HIGHEST)
    scaled = rotated / (values + 0.1)
    return jnp.einsum('tia,qtab,tjb->qtij', basis_in, scaled, basis_out, precision=lax.Precision.HIGHEST)


def reference(store, queries, owner, eig_in, eig_out, eig_val, query_order):
    basis_in = jnp.take(eig_in, owner, axis=0)
    basis_out = jnp.take(eig_out, owner, axis=0)
    values = jnp.take(eig_val, owner, axis=0)
    grads = queries.reshape(NQ, LAYERS, A, B)
    ready = precondition(grads, basis_in, basis_out, values).reshape(NQ, LAYERS * A * B).astype(jnp.bfloat16)
    ordered = jnp.take(ready, query_order, axis=0)
    return lax.dot_general(store, ordered, (((1,), (1,)), ((), ())), preferred_element_type=jnp.float32)
```

```python
import jax
import jax.numpy as jnp
from jax import lax
from jax.sharding import PartitionSpec as P

A = 32
B = 64


def precondition(grads, basis_in, basis_out, values):
    rotated = jnp.einsum(
        "tai,qtab,tbj->qtij", basis_in, grads, basis_out, precision=lax.Precision.HIGHEST
    )
    scaled = rotated / (values + 0.1)
    return jnp.einsum(
        "tia,qtab,tjb->qtij", basis_in, scaled, basis_out, precision=lax.Precision.HIGHEST
    )


def on_device(store, queries, owner, eig_in, eig_out, eig_val, query_order):
    width = A * B
    slots_here = store.shape[1] // width
    slot_ids = lax.axis_index("layer") * slots_here + jnp.arange(slots_here, dtype=jnp.int32)
    model_ids = jnp.take(owner, slot_ids, axis=0)
    basis_in = jnp.take(eig_in, model_ids, axis=0)
    basis_out = jnp.take(eig_out, model_ids, axis=0)
    values = jnp.take(eig_val, model_ids, axis=0)
    grads = queries.reshape(queries.shape[0], slots_here, A, B)
    ready = (
        precondition(grads, basis_in, basis_out, values)
        .reshape(queries.shape[0], slots_here * width)
        .astype(jnp.bfloat16)
    )
    ready = lax.all_gather(ready, "seq", axis=0, tiled=True)
    ordered = jnp.take(ready, query_order, axis=0)
    return lax.psum_scatter(
        lax.dot_general(
            store, ordered, (((1,), (1,)), ((), ())), preferred_element_type=jnp.float32
        ),
        "layer",
        scatter_dimension=0,
        tiled=True,
    )


def solution(mesh):
    in_specs = (P(("parts", "seq"), "layer"), P("seq", "layer"), P(), P(), P(), P(), P())
    out_specs = P(("parts", "seq", "layer"), None)
    return jax.shard_map(
        on_device, mesh=mesh, in_specs=in_specs, out_specs=out_specs, check_vma=False
    )
```

```python
import functools

import jax
import jax.numpy as jnp
from jax import lax
from jax.experimental import pallas as pl
from jax.experimental.pallas import tpu as pltpu
from jax.sharding import PartitionSpec as P

A = 32
B = 64
WIDTH = A * B
LANES = 2 * B
PAIRS = A // 2
CHUNK = 16
GROUP = 4
MESH = pl.DeviceIdType.MESH
EXACT = lax.Precision.HIGHEST


def split(x):
    high = x.astype(jnp.bfloat16)
    return high, (x - high.astype(jnp.float32)).astype(jnp.bfloat16)


def kernel(
    sizes, owner, store, queries, eig_in, eig_out, eig_val, order, out,
    raw, held, ready, mix_in, mix_back, both, small, inverse, wide, narrow, total, stage, sums, perm,
    raw_sem, held_sem, up_sem, down_sem, side_sem, arrive, part_sem, part_arrive,
):
    n_parts, n_seq, n_layer = sizes
    rows = queries.shape[0]
    n_chunks = rows // CHUNK
    block = out.shape[0]
    mine = lax.axis_index("parts")
    here = lax.axis_index("seq")
    layer = lax.axis_index("layer")
    other = 1 - mine

    barrier = pltpu.get_barrier_semaphore()

    def greet(**where):
        pl.semaphore_signal(barrier, inc=1, device_id=where, device_id_type=MESH)

    @pl.when(here > 0)
    def _():
        greet(seq=here - 1)

    @pl.when(here < n_seq - 1)
    def _():
        greet(seq=here + 1)

    greet(parts=other)
    for step in range(1, n_layer):
        greet(layer=lax.rem(layer + step, n_layer))

    def fetch(n):
        slot = jnp.where(n < n_chunks, mine, other)
        piece = (
            pl.ds(pl.multiple_of(lax.rem(n, n_chunks) * CHUNK, CHUNK), CHUNK),
            pl.ds(pl.multiple_of(slot * WIDTH, WIDTH), WIDTH),
        )
        return pltpu.make_async_copy(queries.at[piece], raw.at[n], raw_sem.at[n])

    for n in range(2 * n_chunks):
        fetch(n).start()
    fetch_store = pltpu.make_async_copy(store, held, held_sem)
    fetch_store.start()

    def setup(slot):
        model = owner[layer * 2 + slot]
        basis_in = eig_in[model]
        basis_out = eig_out[model]
        spread = (
            lax.shift_right_logical(lax.broadcasted_iota(jnp.int32, (A, WIDTH), 1), 6)
            == lax.broadcasted_iota(jnp.int32, (A, WIDTH), 0)
        ).astype(jnp.float32)
        mix_in[slot] = jnp.dot(basis_in, spread, precision=EXACT, preferred_element_type=jnp.float32)
        mix_back[slot] = lax.dot_general(
            basis_in, spread, (((0,), (0,)), ((), ())), precision=EXACT,
            preferred_element_type=jnp.float32,
        )
        twice = (
            lax.broadcasted_iota(jnp.int32, (B, LANES), 1) & (B - 1)
            == lax.broadcasted_iota(jnp.int32, (B, LANES), 0)
        ).astype(jnp.float32)
        both[slot] = jnp.zeros(both.shape[1:], both.dtype)
        small[slot] = jnp.zeros(small.shape[1:], small.dtype)
        for way, dims in enumerate((1, 0)):
            doubled = lax.dot_general(
                basis_out, twice, (((dims,), (0,)), ((), ())), precision=EXACT,
                preferred_element_type=jnp.float32,
            )
            high, low = split(doubled)
            for at in range(2):
                column = pl.ds(at * LANES, LANES)
                both[slot, way, pl.ds(at * B, B), column] = high
                both[slot, way, pl.ds(LANES + at * B, B), column] = high
                small[slot, way, pl.ds(at * B, B), column] = low
        values = jnp.dot(
            1.0 / (eig_val[model] + 0.1), twice, precision=EXACT, preferred_element_type=jnp.float32
        )
        pair = lax.broadcasted_iota(jnp.int32, (PAIRS, A), 0) * 2
        slots = lax.broadcasted_iota(jnp.int32, (PAIRS, A), 1)
        even = jnp.dot((slots == pair).astype(jnp.float32), values, precision=EXACT,
                       preferred_element_type=jnp.float32)
        odd = jnp.dot((slots == pair + 1).astype(jnp.float32), values, precision=EXACT,
                      preferred_element_type=jnp.float32)
        lane = lax.broadcasted_iota(jnp.int32, (PAIRS, LANES), 1)
        inverse[slot] = jnp.where(lane < B, even, odd)

    def rotate(x, slot, way):
        high, low = split(x)
        wide[...] = jnp.dot(
            jnp.concatenate([high, low], axis=1), both[slot, way], preferred_element_type=jnp.float32
        ) + jnp.dot(high, small[slot, way], preferred_element_type=jnp.float32)

    def mix(weights, slot, first):
        sums_of = [None] * GROUP
        for a in range(A):
            y = wide[pl.ds(CHUNK * (a // 2), CHUNK), pl.ds(LANES * (a % 2), LANES)]
            for g in range(GROUP):
                w = weights[slot, pl.ds(a, 1), pl.ds(pl.multiple_of((first + g) * LANES, LANES), LANES)]
                term = w * y
                sums_of[g] = term if a == 0 else sums_of[g] + term
        return sums_of

    def at_rows(source, k):
        return pl.ds(pl.multiple_of(source * rows + k * CHUNK, CHUNK), CHUNK)

    def precondition(slot, n, k):
        x = jnp.concatenate(
            [raw[n, :, pl.ds(c * LANES, LANES)] for c in range(PAIRS)], axis=0
        )
        rotate(x, slot, 0)

        def inner(i, _):
            for g, value in enumerate(mix(mix_in, slot, i * GROUP)):
                pair = i * GROUP + g
                narrow[pl.ds(pl.multiple_of(pair * CHUNK, CHUNK), CHUNK), :] = (
                    value * inverse[slot, pl.ds(pair, 1), :]
                )
            return 0

        lax.fori_loop(0, PAIRS // GROUP, inner, 0)
        rotate(narrow[...], slot, 1)

        def outer(i, _):
            for g, value in enumerate(mix(mix_back, slot, i * GROUP)):
                column = pl.ds(pl.multiple_of((i * GROUP + g) * LANES, LANES), LANES)
                ready[slot, at_rows(here, k), column] = value.astype(jnp.bfloat16)
            return 0

        lax.fori_loop(0, PAIRS // GROUP, outer, 0)

    def send(source, k, sems, **where):
        piece = ready.at[mine, at_rows(source, k), :]
        return pltpu.make_async_remote_copy(
            src_ref=piece, dst_ref=piece, send_sem=sems.at[source, k],
            recv_sem=arrive.at[mine, source, k], device_id=where, device_id_type=MESH,
        )

    def to_up(source, k):
        return send(source, k, up_sem, seq=here + 1)

    def to_down(source, k):
        return send(source, k, down_sem, seq=here - 1)

    def to_side(source, k):
        return send(source, k, side_sem, parts=other)

    def await_piece(slot, source, k):
        piece = ready.at[slot, at_rows(source, k), :]
        pltpu.make_async_remote_copy(
            src_ref=piece, dst_ref=piece, send_sem=side_sem.at[source, k],
            recv_sem=arrive.at[slot, source, k], device_id={"parts": other}, device_id_type=MESH,
        ).wait_recv()

    def pass_on(distance, k):
        below, above = here - distance, here + distance

        @pl.when(below >= 0)
        def _():
            await_piece(mine, below, k)

            @pl.when(here < n_seq - 1)
            def _():
                to_up(below, k).start()

            to_side(below, k).start()

        @pl.when(above < n_seq)
        def _():
            await_piece(mine, above, k)

            @pl.when(here > 0)
            def _():
                to_down(above, k).start()

            to_side(above, k).start()

    n_greetings = (
        jnp.where(here > 0, 1, 0) + jnp.where(here < n_seq - 1, 1, 0) + n_layer
    )

    def job(n, _):
        k = lax.rem(n, n_chunks)
        slot = jnp.where(n < n_chunks, mine, other)

        @pl.when(k == 0)
        def _():
            setup(slot)

        fetch(n).wait()
        precondition(slot, n, k)

        @pl.when(n == 0)
        def _():
            pl.semaphore_wait(barrier, n_greetings)

        @pl.when(n < n_chunks)
        def _():
            @pl.when(here < n_seq - 1)
            def _():
                to_up(here, k).start()

            @pl.when(here > 0)
            def _():
                to_down(here, k).start()

        @pl.when(n >= n_chunks)
        def _():
            pass_on(1, k)

        return 0

    lax.fori_loop(0, 2 * n_chunks, job, 0)

    which = lax.broadcasted_iota(jnp.int32, perm.shape, 0)
    perm[...] = (which == order[...].reshape(1, perm.shape[1])).astype(jnp.bfloat16)

    def relay(n, _):
        pass_on(2 + n // n_chunks, lax.rem(n, n_chunks))
        return 0

    lax.fori_loop(0, (n_seq - 2) * n_chunks, relay, 0)

    def score(slot):
        return lax.dot_general(
            held[:, pl.ds(pl.multiple_of(slot * WIDTH, WIDTH), WIDTH)], ready[slot],
            (((1,), (1,)), ((), ())), preferred_element_type=jnp.float32,
        )

    fetch_store.wait()
    total[...] = score(mine)

    def each_source(do):
        def body(n, _):
            source = n // n_chunks

            @pl.when(source != here)
            def _():
                do(source, lax.rem(n, n_chunks))

            return 0

        lax.fori_loop(0, n_seq * n_chunks, body, 0)

    each_source(lambda source, k: await_piece(other, source, k))
    total[...] += score(other)

    stage[...] = total[...].astype(jnp.bfloat16)

    def part(step):
        to = lax.rem(layer + step, n_layer)
        return pltpu.make_async_remote_copy(
            src_ref=stage.at[pl.ds(pl.multiple_of(to * block, CHUNK), block), :],
            dst_ref=sums.at[step - 1], send_sem=part_sem.at[step - 1],
            recv_sem=part_arrive.at[step - 1], device_id={"layer": to}, device_id_type=MESH,
        )

    for step in range(1, n_layer):
        part(step).start()

    each_source(lambda source, k: to_side(source, k).wait_send())

    def drain(n, _):
        source, k = n // n_chunks, lax.rem(n, n_chunks)

        @pl.when((source <= here) & (here < n_seq - 1))
        def _():
            to_up(source, k).wait_send()

        @pl.when((source >= here) & (here > 0))
        def _():
            to_down(source, k).wait_send()

        return 0

    lax.fori_loop(0, n_seq * n_chunks, drain, 0)

    result = total[pl.ds(pl.multiple_of(layer * block, CHUNK), block), :]
    for step in range(1, n_layer):
        part(step).wait_recv()
        result = result + sums[step - 1].astype(jnp.float32)
    high, low = split(result)
    lowest = (result - high.astype(jnp.float32) - low.astype(jnp.float32)).astype(jnp.bfloat16)
    out[...] = sum(
        jnp.dot(piece, perm[...], preferred_element_type=jnp.float32) for piece in (lowest, low, high)
    )
    for step in range(1, n_layer):
        part(step).wait_send()


def on_device(sizes, store, queries, owner, eig_in, eig_out, eig_val, query_order):
    n_parts, n_seq, n_layer = sizes
    rows = queries.shape[0]
    n_queries = rows * n_seq
    n_store = store.shape[0]
    n_chunks = rows // CHUNK
    slots = store.shape[1] // WIDTH
    assert slots == 2 and n_parts == 2 and rows % CHUNK == 0
    block = n_store // n_layer
    vmem = pl.BlockSpec(memory_space=pltpu.VMEM)
    anywhere = pl.BlockSpec(memory_space=pl.ANY)
    f32, bf16 = jnp.float32, jnp.bfloat16
    dma = pltpu.SemaphoreType.DMA
    return pl.pallas_call(
        functools.partial(kernel, sizes),
        out_shape=jax.ShapeDtypeStruct((block, n_queries), f32),
        in_specs=[pl.BlockSpec(memory_space=pltpu.SMEM), anywhere, anywhere, vmem, vmem, vmem, vmem],
        out_specs=vmem,
        scratch_shapes=[
            pltpu.VMEM((slots * n_chunks, CHUNK, WIDTH), f32),
            pltpu.VMEM(store.shape, bf16),
            pltpu.VMEM((slots, n_queries, WIDTH), bf16),
            pltpu.VMEM((slots, A, WIDTH), f32),
            pltpu.VMEM((slots, A, WIDTH), f32),
            pltpu.VMEM((slots, 2, 2 * LANES, 2 * LANES), bf16),
            pltpu.VMEM((slots, 2, LANES, 2 * LANES), bf16),
            pltpu.VMEM((slots, PAIRS, LANES), f32),
            pltpu.VMEM((PAIRS * CHUNK, 2 * LANES), f32),
            pltpu.VMEM((PAIRS * CHUNK, LANES), f32),
            pltpu.VMEM((n_store, n_queries), f32),
            pltpu.VMEM((n_store, n_queries), bf16),
            pltpu.VMEM((n_layer - 1, block, n_queries), bf16),
            pltpu.VMEM((n_queries, n_queries), bf16),
            dma((slots * n_chunks,)),
            dma,
            dma((n_seq, n_chunks)),
            dma((n_seq, n_chunks)),
            dma((n_seq, n_chunks)),
            dma((slots, n_seq, n_chunks)),
            dma((n_layer - 1,)),
            dma((n_layer - 1,)),
        ],
        compiler_params=pltpu.CompilerParams(
            collective_id=0, has_side_effects=True, vmem_limit_bytes=48 * 1024 * 1024
        ),
        name="gather_score",
    )(owner, store, queries, eig_in, eig_out, eig_val, query_order)


def solution(mesh):
    sizes = tuple(mesh.shape[axis] for axis in ("parts", "seq", "layer"))
    in_specs = (P(("parts", "seq"), "layer"), P("seq", "layer"), P(), P(), P(), P(), P())
    out_specs = P(("parts", "seq", "layer"), None)
    return jax.shard_map(
        functools.partial(on_device, sizes), mesh=mesh, in_specs=in_specs, out_specs=out_specs,
        check_vma=False,
    )
```

```python
import functools

import jax
import jax.numpy as jnp
from jax import lax
from jax.experimental import pallas as pl
from jax.experimental.pallas import tpu as pltpu
from jax.sharding import PartitionSpec as P

A = 32
B = 64
WIDTH = A * B
LANES = 2 * B
PAIRS = A // 2
CHUNK = 16
GROUP = 4
MESH = pl.DeviceIdType.MESH
EXACT = lax.Precision.HIGHEST


def split(x):
    high = x.astype(jnp.bfloat16)
    return high, (x - high.astype(jnp.float32)).astype(jnp.bfloat16)


def kernel(
    sizes, owner_at, store, queries, eig_in_at, eig_out_at, eig_val_at, order_at, out,
    owner, eig_in, eig_out, eig_val, order, small_sem, raw, held, ready, mix_in, mix_back, both, small, inverse, wide, narrow, total, stage, sums, perm,
    raw_sem, held_sem, up_sem, down_sem, side_sem, arrive, part_sem, part_arrive,
):
    n_parts, n_seq, n_layer = sizes
    rows = queries.shape[0]
    n_chunks = rows // CHUNK
    block = out.shape[0]
    mine = lax.axis_index("parts")
    here = lax.axis_index("seq")
    layer = lax.axis_index("layer")
    other = 1 - mine

    barrier = pltpu.get_barrier_semaphore()

    def greet(**where):
        pl.semaphore_signal(barrier, inc=1, device_id=where, device_id_type=MESH)

    @pl.when(here > 0)
    def _():
        greet(seq=here - 1)

    @pl.when(here < n_seq - 1)
    def _():
        greet(seq=here + 1)

    greet(parts=other)
    for step in range(1, n_layer):
        greet(layer=lax.rem(layer + step, n_layer))

    def fetch(n):
        slot = jnp.where(n < n_chunks, mine, other)
        piece = (
            pl.ds(pl.multiple_of(lax.rem(n, n_chunks) * CHUNK, CHUNK), CHUNK),
            pl.ds(pl.multiple_of(slot * WIDTH, WIDTH), WIDTH),
        )
        return pltpu.make_async_copy(queries.at[piece], raw.at[n], raw_sem.at[n])

    tables = [
        pltpu.make_async_copy(source, target, small_sem.at[i])
        for i, (source, target) in enumerate((
            (owner_at, owner), (eig_in_at, eig_in), (eig_out_at, eig_out), (eig_val_at, eig_val),
            (order_at, order),
        ))
    ]
    for table in tables:
        table.start()
    for n in range(2 * n_chunks):
        fetch(n).start()
    fetch_store = pltpu.make_async_copy(store, held, held_sem)
    fetch_store.start()

    for table in tables:
        table.wait()

    def setup(slot):
        model = owner[layer * 2 + slot]
        basis_in = eig_in[model]
        basis_out = eig_out[model]
        spread = (
            lax.shift_right_logical(lax.broadcasted_iota(jnp.int32, (A, WIDTH), 1), 6)
            == lax.broadcasted_iota(jnp.int32, (A, WIDTH), 0)
        ).astype(jnp.float32)
        mix_in[slot] = jnp.dot(basis_in, spread, precision=EXACT, preferred_element_type=jnp.float32)
        mix_back[slot] = lax.dot_general(
            basis_in, spread, (((0,), (0,)), ((), ())), precision=EXACT,
            preferred_element_type=jnp.float32,
        )
        twice = (
            lax.broadcasted_iota(jnp.int32, (B, LANES), 1) & (B - 1)
            == lax.broadcasted_iota(jnp.int32, (B, LANES), 0)
        ).astype(jnp.float32)
        both[slot] = jnp.zeros(both.shape[1:], both.dtype)
        small[slot] = jnp.zeros(small.shape[1:], small.dtype)
        for way, dims in enumerate((1, 0)):
            doubled = lax.dot_general(
                basis_out, twice, (((dims,), (0,)), ((), ())), precision=EXACT,
                preferred_element_type=jnp.float32,
            )
            high, low = split(doubled)
            for at in range(2):
                column = pl.ds(at * LANES, LANES)
                both[slot, way, pl.ds(at * B, B), column] = high
                both[slot, way, pl.ds(LANES + at * B, B), column] = high
                small[slot, way, pl.ds(at * B, B), column] = low
        values = jnp.dot(
            1.0 / (eig_val[model] + 0.1), twice, precision=EXACT, preferred_element_type=jnp.float32
        )
        pair = lax.broadcasted_iota(jnp.int32, (PAIRS, A), 0) * 2
        slots = lax.broadcasted_iota(jnp.int32, (PAIRS, A), 1)
        even = jnp.dot((slots == pair).astype(jnp.float32), values, precision=EXACT,
                       preferred_element_type=jnp.float32)
        odd = jnp.dot((slots == pair + 1).astype(jnp.float32), values, precision=EXACT,
                      preferred_element_type=jnp.float32)
        lane = lax.broadcasted_iota(jnp.int32, (PAIRS, LANES), 1)
        inverse[slot] = jnp.where(lane < B, even, odd)

    def rotate(x, slot, way):
        high, low = split(x)
        wide[...] = jnp.dot(
            jnp.concatenate([high, low], axis=1), both[slot, way], preferred_element_type=jnp.float32
        ) + jnp.dot(high, small[slot, way], preferred_element_type=jnp.float32)

    def mix(weights, slot, first):
        sums_of = [None] * GROUP
        for a in range(A):
            y = wide[pl.ds(CHUNK * (a // 2), CHUNK), pl.ds(LANES * (a % 2), LANES)]
            for g in range(GROUP):
                w = weights[slot, pl.ds(a, 1), pl.ds(pl.multiple_of((first + g) * LANES, LANES), LANES)]
                term = w * y
                sums_of[g] = term if a == 0 else sums_of[g] + term
        return sums_of

    def at_rows(source, k):
        return pl.ds(pl.multiple_of(source * rows + k * CHUNK, CHUNK), CHUNK)

    def precondition(slot, n, k):
        x = jnp.concatenate(
            [raw[n, :, pl.ds(c * LANES, LANES)] for c in range(PAIRS)], axis=0
        )
        rotate(x, slot, 0)

        def inner(i, _):
            for g, value in enumerate(mix(mix_in, slot, i * GROUP)):
                pair = i * GROUP + g
                narrow[pl.ds(pl.multiple_of(pair * CHUNK, CHUNK), CHUNK), :] = (
                    value * inverse[slot, pl.ds(pair, 1), :]
                )
            return 0

        lax.fori_loop(0, PAIRS // GROUP, inner, 0)
        rotate(narrow[...], slot, 1)

        def outer(i, _):
            for g, value in enumerate(mix(mix_back, slot, i * GROUP)):
                column = pl.ds(pl.multiple_of((i * GROUP + g) * LANES, LANES), LANES)
                ready[slot, at_rows(here, k), column] = value.astype(jnp.bfloat16)
            return 0

        lax.fori_loop(0, PAIRS // GROUP, outer, 0)

    def send(source, k, sems, **where):
        piece = ready.at[mine, at_rows(source, k), :]
        return pltpu.make_async_remote_copy(
            src_ref=piece, dst_ref=piece, send_sem=sems.at[source, k],
            recv_sem=arrive.at[mine, source, k], device_id=where, device_id_type=MESH,
        )

    def to_up(source, k):
        return send(source, k, up_sem, seq=here + 1)

    def to_down(source, k):
        return send(source, k, down_sem, seq=here - 1)

    def to_side(source, k):
        return send(source, k, side_sem, parts=other)

    def await_piece(slot, source, k):
        piece = ready.at[slot, at_rows(source, k), :]
        pltpu.make_async_remote_copy(
            src_ref=piece, dst_ref=piece, send_sem=side_sem.at[source, k],
            recv_sem=arrive.at[slot, source, k], device_id={"parts": other}, device_id_type=MESH,
        ).wait_recv()

    def pass_on(distance, k):
        below, above = here - distance, here + distance

        @pl.when(below >= 0)
        def _():
            await_piece(mine, below, k)

            @pl.when(here < n_seq - 1)
            def _():
                to_up(below, k).start()

            to_side(below, k).start()

        @pl.when(above < n_seq)
        def _():
            await_piece(mine, above, k)

            @pl.when(here > 0)
            def _():
                to_down(above, k).start()

            to_side(above, k).start()

    n_greetings = (
        jnp.where(here > 0, 1, 0) + jnp.where(here < n_seq - 1, 1, 0) + n_layer
    )

    def job(n, _):
        k = lax.rem(n, n_chunks)
        slot = jnp.where(n < n_chunks, mine, other)

        @pl.when(k == 0)
        def _():
            setup(slot)

        fetch(n).wait()
        precondition(slot, n, k)

        @pl.when(n == 0)
        def _():
            pl.semaphore_wait(barrier, n_greetings)

        @pl.when(n < n_chunks)
        def _():
            @pl.when(here < n_seq - 1)
            def _():
                to_up(here, k).start()

            @pl.when(here > 0)
            def _():
                to_down(here, k).start()

        @pl.when(n >= n_chunks)
        def _():
            pass_on(1, k)

        return 0

    lax.fori_loop(0, 2 * n_chunks, job, 0)

    which = lax.broadcasted_iota(jnp.int32, perm.shape, 0)
    perm[...] = (which == order[...].reshape(1, perm.shape[1])).astype(jnp.bfloat16)

    def relay(n, _):
        pass_on(2 + n // n_chunks, lax.rem(n, n_chunks))
        return 0

    lax.fori_loop(0, (n_seq - 2) * n_chunks, relay, 0)

    def score(slot):
        return lax.dot_general(
            held[:, pl.ds(pl.multiple_of(slot * WIDTH, WIDTH), WIDTH)], ready[slot],
            (((1,), (1,)), ((), ())), preferred_element_type=jnp.float32,
        )

    fetch_store.wait()
    total[...] = score(mine)

    def each_source(do):
        def body(n, _):
            source = n // n_chunks

            @pl.when(source != here)
            def _():
                do(source, lax.rem(n, n_chunks))

            return 0

        lax.fori_loop(0, n_seq * n_chunks, body, 0)

    each_source(lambda source, k: await_piece(other, source, k))
    total[...] += score(other)

    stage[...] = total[...].astype(jnp.bfloat16)

    def part(step):
        to = lax.rem(layer + step, n_layer)
        return pltpu.make_async_remote_copy(
            src_ref=stage.at[pl.ds(pl.multiple_of(to * block, CHUNK), block), :],
            dst_ref=sums.at[step - 1], send_sem=part_sem.at[step - 1],
            recv_sem=part_arrive.at[step - 1], device_id={"layer": to}, device_id_type=MESH,
        )

    for step in range(1, n_layer):
        part(step).start()

    each_source(lambda source, k: to_side(source, k).wait_send())

    def drain(n, _):
        source, k = n // n_chunks, lax.rem(n, n_chunks)

        @pl.when((source <= here) & (here < n_seq - 1))
        def _():
            to_up(source, k).wait_send()

        @pl.when((source >= here) & (here > 0))
        def _():
            to_down(source, k).wait_send()

        return 0

    lax.fori_loop(0, n_seq * n_chunks, drain, 0)

    result = total[pl.ds(pl.multiple_of(layer * block, CHUNK), block), :]
    for step in range(1, n_layer):
        part(step).wait_recv()
        result = result + sums[step - 1].astype(jnp.float32)
    high, low = split(result)
    lowest = (result - high.astype(jnp.float32) - low.astype(jnp.float32)).astype(jnp.bfloat16)
    out[...] = sum(
        jnp.dot(piece, perm[...], preferred_element_type=jnp.float32) for piece in (lowest, low, high)
    )
    for step in range(1, n_layer):
        part(step).wait_send()


def on_device(sizes, store, queries, owner, eig_in, eig_out, eig_val, query_order):
    n_parts, n_seq, n_layer = sizes
    rows = queries.shape[0]
    n_queries = rows * n_seq
    n_store = store.shape[0]
    n_chunks = rows // CHUNK
    slots = store.shape[1] // WIDTH
    assert slots == 2 and n_parts == 2 and rows % CHUNK == 0
    block = n_store // n_layer
    vmem = pl.BlockSpec(memory_space=pltpu.VMEM)
    anywhere = pl.BlockSpec(memory_space=pl.ANY)
    f32, bf16 = jnp.float32, jnp.bfloat16
    dma = pltpu.SemaphoreType.DMA
    return pl.pallas_call(
        functools.partial(kernel, sizes),
        out_shape=jax.ShapeDtypeStruct((block, n_queries), f32),
        in_specs=[anywhere] * 7,
        out_specs=vmem,
        scratch_shapes=[
            pltpu.SMEM(owner.shape, owner.dtype),
            pltpu.VMEM(eig_in.shape, f32),
            pltpu.VMEM(eig_out.shape, f32),
            pltpu.VMEM(eig_val.shape, f32),
            pltpu.VMEM(query_order.shape, query_order.dtype),
            dma((5,)),
            pltpu.VMEM((slots * n_chunks, CHUNK, WIDTH), f32),
            pltpu.VMEM(store.shape, bf16),
            pltpu.VMEM((slots, n_queries, WIDTH), bf16),
            pltpu.VMEM((slots, A, WIDTH), f32),
            pltpu.VMEM((slots, A, WIDTH), f32),
            pltpu.VMEM((slots, 2, 2 * LANES, 2 * LANES), bf16),
            pltpu.VMEM((slots, 2, LANES, 2 * LANES), bf16),
            pltpu.VMEM((slots, PAIRS, LANES), f32),
            pltpu.VMEM((PAIRS * CHUNK, 2 * LANES), f32),
            pltpu.VMEM((PAIRS * CHUNK, LANES), f32),
            pltpu.VMEM((n_store, n_queries), f32),
            pltpu.VMEM((n_store, n_queries), bf16),
            pltpu.VMEM((n_layer - 1, block, n_queries), bf16),
            pltpu.VMEM((n_queries, n_queries), bf16),
            dma((slots * n_chunks,)),
            dma,
            dma((n_seq, n_chunks)),
            dma((n_seq, n_chunks)),
            dma((n_seq, n_chunks)),
            dma((slots, n_seq, n_chunks)),
            dma((n_layer - 1,)),
            dma((n_layer - 1,)),
        ],
        compiler_params=pltpu.CompilerParams(
            collective_id=0, has_side_effects=True, vmem_limit_bytes=60 * 1024 * 1024
        ),
        name="gather_score",
    )(owner, store, queries, eig_in, eig_out, eig_val, query_order)


def solution(mesh):
    sizes = tuple(mesh.shape[axis] for axis in ("parts", "seq", "layer"))
    in_specs = (P(("parts", "seq"), "layer"), P("seq", "layer"), P(), P(), P(), P(), P())
    out_specs = P(("parts", "seq", "layer"), None)
    return jax.shard_map(
        functools.partial(on_device, sizes), mesh=mesh, in_specs=in_specs, out_specs=out_specs,
        check_vma=False,
    )
```

```python
import functools

import jax
import jax.numpy as jnp
from jax import lax
from jax.experimental import pallas as pl
from jax.experimental.pallas import tpu as pltpu
from jax.sharding import PartitionSpec as P

A = 32
B = 64
WIDTH = A * B
LANES = 2 * B
PAIRS = A // 2
CHUNK = 16
GROUP = 16
HALVES = 1
SPREAD = 2
MESH = pl.DeviceIdType.MESH
EXACT = lax.Precision.HIGHEST


def split(x):
    high = x.astype(jnp.bfloat16)
    return high, (x - high.astype(jnp.float32)).astype(jnp.bfloat16)


def kernel(
    sizes, owner_at, store, queries, eig_in_at, eig_out_at, eig_val_at, order_at, out,
    owner, eig_in, eig_out, eig_val, order, small_sem, raw, held, ready, mix_in, mix_back, both, small, inverse, wide, narrow, total, stage, sums, perm,
    raw_sem, held_sem, up_sem, down_sem, side_sem, arrive, side_arrive, part_sem, part_arrive,
):
    n_parts, n_seq, n_layer = sizes
    rows = queries.shape[0]
    n_chunks = rows // CHUNK
    block = out.shape[0]
    mine = lax.axis_index("parts")
    here = lax.axis_index("seq")
    layer = lax.axis_index("layer")
    other = 1 - mine

    barrier = pltpu.get_barrier_semaphore()

    def greet(**where):
        pl.semaphore_signal(barrier, inc=1, device_id=where, device_id_type=MESH)

    @pl.when(here > 0)
    def _():
        greet(seq=here - 1)

    @pl.when(here < n_seq - 1)
    def _():
        greet(seq=here + 1)

    greet(parts=other)
    for step in range(1, n_layer):
        greet(layer=lax.rem(layer + step, n_layer))

    def chunk_of(n):
        return jnp.where(n < n_chunks, n, 2 * n_chunks - 1 - n)

    def fetch(n):
        slot = jnp.where(n < n_chunks, mine, other)
        piece = (
            pl.ds(pl.multiple_of(chunk_of(n) * CHUNK, CHUNK), CHUNK),
            pl.ds(pl.multiple_of(slot * WIDTH, WIDTH), WIDTH),
        )
        return pltpu.make_async_copy(queries.at[piece], raw.at[n], raw_sem.at[n])

    tables = [
        pltpu.make_async_copy(source, target, small_sem.at[i])
        for i, (source, target) in enumerate((
            (owner_at, owner), (eig_in_at, eig_in), (eig_out_at, eig_out), (eig_val_at, eig_val),
            (order_at, order),
        ))
    ]
    for table in tables:
        table.start()
    for n in range(2 * n_chunks):
        fetch(n).start()
    fetch_store = pltpu.make_async_copy(store, held, held_sem)
    fetch_store.start()

    for table in tables:
        table.wait()

    def setup(slot):
        model = owner[layer * 2 + slot]
        basis_in = eig_in[model]
        basis_out = eig_out[model]
        spread = (
            lax.shift_right_logical(lax.broadcasted_iota(jnp.int32, (A, WIDTH), 1), 6)
            == lax.broadcasted_iota(jnp.int32, (A, WIDTH), 0)
        ).astype(jnp.float32)
        mix_in[slot] = jnp.dot(basis_in, spread, precision=EXACT, preferred_element_type=jnp.float32)
        mix_back[slot] = lax.dot_general(
            basis_in, spread, (((0,), (0,)), ((), ())), precision=EXACT,
            preferred_element_type=jnp.float32,
        )
        twice = (
            lax.broadcasted_iota(jnp.int32, (B, LANES), 1) & (B - 1)
            == lax.broadcasted_iota(jnp.int32, (B, LANES), 0)
        ).astype(jnp.float32)
        both[slot] = jnp.zeros(both.shape[1:], both.dtype)
        small[slot] = jnp.zeros(small.shape[1:], small.dtype)
        for way, dims in enumerate((1, 0)):
            doubled = lax.dot_general(
                basis_out, twice, (((dims,), (0,)), ((), ())), precision=EXACT,
                preferred_element_type=jnp.float32,
            )
            high, low = split(doubled)
            for at in range(2):
                column = pl.ds(at * LANES, LANES)
                both[slot, way, pl.ds(at * B, B), column] = high
                both[slot, way, pl.ds(LANES + at * B, B), column] = high
                small[slot, way, pl.ds(at * B, B), column] = low
        values = jnp.dot(
            1.0 / (eig_val[model] + 0.1), twice, precision=EXACT, preferred_element_type=jnp.float32
        )
        pair = lax.broadcasted_iota(jnp.int32, (PAIRS, A), 0) * 2
        slots = lax.broadcasted_iota(jnp.int32, (PAIRS, A), 1)
        even = jnp.dot((slots == pair).astype(jnp.float32), values, precision=EXACT,
                       preferred_element_type=jnp.float32)
        odd = jnp.dot((slots == pair + 1).astype(jnp.float32), values, precision=EXACT,
                      preferred_element_type=jnp.float32)
        lane = lax.broadcasted_iota(jnp.int32, (PAIRS, LANES), 1)
        inverse[slot] = jnp.where(lane < B, even, odd)

    def rotate(x, slot, way):
        high, low = split(x)
        wide[...] = jnp.dot(
            jnp.concatenate([high, low], axis=1), both[slot, way], preferred_element_type=jnp.float32
        ) + jnp.dot(high, small[slot, way], preferred_element_type=jnp.float32)

    def mix(weights, slot, first):
        sums_of = [None] * GROUP
        for a in range(A):
            y = wide[pl.ds(CHUNK * (a // 2), CHUNK), pl.ds(LANES * (a % 2), LANES)]
            for g in range(GROUP):
                w = weights[slot, pl.ds(a, 1), pl.ds(pl.multiple_of((first + g) * LANES, LANES), LANES)]
                term = w * y
                sums_of[g] = term if a == 0 else sums_of[g] + term
        return sums_of

    def at_rows(source, k):
        return pl.ds(pl.multiple_of(source * rows + k * CHUNK, CHUNK), CHUNK)

    def precondition(slot, n, k):
        x = jnp.concatenate(
            [raw[n, :, pl.ds(c * LANES, LANES)] for c in range(PAIRS)], axis=0
        )
        rotate(x, slot, 0)

        def inner(i, _):
            for g, value in enumerate(mix(mix_in, slot, i * GROUP)):
                pair = i * GROUP + g
                narrow[pl.ds(pl.multiple_of(pair * CHUNK, CHUNK), CHUNK), :] = (
                    value * inverse[slot, pl.ds(pair, 1), :]
                )
            return 0

        lax.fori_loop(0, PAIRS // GROUP, inner, 0)
        rotate(narrow[...], slot, 1)

        def outer(i, _):
            for g, value in enumerate(mix(mix_back, slot, i * GROUP)):
                column = pl.ds(pl.multiple_of((i * GROUP + g) * LANES, LANES), LANES)
                ready[slot, at_rows(here, k), column] = value.astype(jnp.bfloat16)
            return 0

        lax.fori_loop(0, PAIRS // GROUP, outer, 0)

    def copy(piece, sem, arrival, **where):
        return pltpu.make_async_remote_copy(
            src_ref=piece, dst_ref=piece, send_sem=sem, recv_sem=arrival,
            device_id=where, device_id_type=MESH,
        )

    def halves(slot, source, k):
        for h in range(HALVES):
            yield (
                ready.at[slot, at_rows(source, k), pl.ds(h * (WIDTH // HALVES), WIDTH // HALVES)],
                arrive.at[slot, source, k, h],
            )

    def go_up(slot, source, piece, arrival):
        @pl.when(here < n_seq - 1)
        def _():
            copy(piece, up_sem.at[slot, source], arrival, seq=here + 1).start()

    def go_down(slot, source, piece, arrival):
        @pl.when(here > 0)
        def _():
            copy(piece, down_sem.at[slot, source], arrival, seq=here - 1).start()

    def pass_on(slot, source, k, is_end, ways):
        for piece, arrival in halves(slot, source, k):
            copy(piece, side_sem.at[source], arrival, parts=other).wait_recv()
            for way in ways:
                way(slot, source, piece, arrival)
            if slot is mine:
                @pl.when(jnp.logical_not(is_end & (k == n_chunks - 1)))
                def _():
                    copy(piece, side_sem.at[source], side_arrive.at[source], parts=other).start()

    def pass_all(n):
        distance, k = 1 + n // (n_chunks + 1), lax.rem(n, n_chunks + 1)
        below, above = here - distance, here + distance
        for source, exists, is_end, way in (
            (below, below >= 0, below == 0, go_up),
            (above, above < n_seq, above == n_seq - 1, go_down),
        ):
            @pl.when(exists & (k < n_chunks))
            def _():
                pass_on(mine, source, k, is_end, (way,))

            @pl.when(exists & (k == n_chunks) & is_end)
            def _():
                pass_on(other, source, n_chunks - 1, is_end, (way,))

    n_greetings = (
        jnp.where(here > 0, 1, 0) + jnp.where(here < n_seq - 1, 1, 0) + n_layer
    )

    which = lax.broadcasted_iota(jnp.int32, perm.shape, 0)
    perm[...] = (which == order[...].reshape(1, perm.shape[1])).astype(jnp.bfloat16)

    def job(n, _):
        slot = jnp.where(n < n_chunks, mine, other)
        late = n - n_chunks
        task = jnp.where(n < n_chunks, n, n_chunks + late // SPREAD)
        due = (n < n_chunks) | ((lax.rem(late, SPREAD) == 0) & (task < 2 * n_chunks))

        @pl.when(n == 1)
        def _():
            pl.semaphore_wait(barrier, n_greetings)

        @pl.when((n >= 1) & (n <= n_chunks))
        def _():
            for piece, arrival in halves(mine, here, n - 1):
                go_up(mine, here, piece, arrival)
                go_down(mine, here, piece, arrival)

        @pl.when((n == n_chunks + 1) & ((here == 0) | (here == n_seq - 1)))
        def _():
            for piece, arrival in halves(other, here, n_chunks - 1):
                go_up(other, here, piece, arrival)
                go_down(other, here, piece, arrival)

        @pl.when((n >= n_chunks) & (n < n_chunks + (n_seq - 1) * (n_chunks + 1)))
        def _():
            pass_all(n - n_chunks)

        @pl.when((n == 0) | (n == n_chunks))
        def _():
            setup(slot)

        @pl.when(due)
        def _():
            fetch(task).wait()
            precondition(slot, task, chunk_of(task))

        return 0

    n_steps = n_chunks + max((n_seq - 1) * (n_chunks + 1), SPREAD * n_chunks)
    lax.fori_loop(0, n_steps, job, 0)

    def score(slot):
        return lax.dot_general(
            held[:, pl.ds(pl.multiple_of(slot * WIDTH, WIDTH), WIDTH)], ready[slot],
            (((1,), (1,)), ((), ())), preferred_element_type=jnp.float32,
        )

    fetch_store.wait()
    total[...] = score(mine)

    def slab(slot, source, size):
        return ready.at[slot, pl.ds(pl.multiple_of(source * rows, CHUNK), size), :]

    def each_source(do):
        def body(source, _):
            @pl.when(source != here)
            def _():
                is_end = (source == 0) | (source == n_seq - 1)

                @pl.when(jnp.logical_not(is_end))
                def _():
                    do(source, rows)

                if rows > CHUNK:
                    @pl.when(is_end)
                    def _():
                        do(source, rows - CHUNK)

            return 0

        lax.fori_loop(0, n_seq, body, 0)

    def side_slab(slot, source, size):
        return copy(slab(slot, source, size), side_sem.at[source], side_arrive.at[source], parts=other)

    each_source(lambda source, size: side_slab(other, source, size).wait_recv())
    total[...] += score(other)

    stage[...] = total[...].astype(jnp.bfloat16)

    def part(step):
        to = lax.rem(layer + step, n_layer)
        return pltpu.make_async_remote_copy(
            src_ref=stage.at[pl.ds(pl.multiple_of(to * block, CHUNK), block), :],
            dst_ref=sums.at[step - 1], send_sem=part_sem.at[step - 1],
            recv_sem=part_arrive.at[step - 1], device_id={"layer": to}, device_id_type=MESH,
        )

    for step in range(1, n_layer):
        part(step).start()

    each_source(lambda source, size: side_slab(mine, source, size).wait_send())

    def drain(source, _):
        for comes, has_next, sems, where, is_end in (
            (source <= here, here < n_seq - 1, up_sem, here + 1, source == 0),
            (source >= here, here > 0, down_sem, here - 1, source == n_seq - 1),
        ):
            @pl.when(comes & has_next)
            def _():
                copy(slab(mine, source, rows), sems.at[mine, source], arrive.at[mine, source, 0, 0],
                     seq=where).wait_send()

            @pl.when(comes & has_next & is_end)
            def _():
                copy(slab(other, source, CHUNK), sems.at[other, source],
                     arrive.at[other, source, 0, 0], seq=where).wait_send()

        return 0

    lax.fori_loop(0, n_seq, drain, 0)

    result = total[pl.ds(pl.multiple_of(layer * block, CHUNK), block), :]
    for step in range(1, n_layer):
        part(step).wait_recv()
        result = result + sums[step - 1].astype(jnp.float32)
    high, low = split(result)
    lowest = (result - high.astype(jnp.float32) - low.astype(jnp.float32)).astype(jnp.bfloat16)
    out[...] = sum(
        jnp.dot(piece, perm[...], preferred_element_type=jnp.float32) for piece in (lowest, low, high)
    )
    for step in range(1, n_layer):
        part(step).wait_send()


def on_device(sizes, store, queries, owner, eig_in, eig_out, eig_val, query_order):
    n_parts, n_seq, n_layer = sizes
    rows = queries.shape[0]
    n_queries = rows * n_seq
    n_store = store.shape[0]
    n_chunks = rows // CHUNK
    slots = store.shape[1] // WIDTH
    assert slots == 2 and n_parts == 2 and rows % CHUNK == 0
    block = n_store // n_layer
    vmem = pl.BlockSpec(memory_space=pltpu.VMEM)
    anywhere = pl.BlockSpec(memory_space=pl.ANY)
    f32, bf16 = jnp.float32, jnp.bfloat16
    dma = pltpu.SemaphoreType.DMA
    return pl.pallas_call(
        functools.partial(kernel, sizes),
        out_shape=jax.ShapeDtypeStruct((block, n_queries), f32),
        in_specs=[anywhere] * 7,
        out_specs=vmem,
        scratch_shapes=[
            pltpu.SMEM(owner.shape, owner.dtype),
            pltpu.VMEM(eig_in.shape, f32),
            pltpu.VMEM(eig_out.shape, f32),
            pltpu.VMEM(eig_val.shape, f32),
            pltpu.VMEM(query_order.shape, query_order.dtype),
            dma((5,)),
            pltpu.VMEM((slots * n_chunks, CHUNK, WIDTH), f32),
            pltpu.VMEM(store.shape, bf16),
            pltpu.VMEM((slots, n_queries, WIDTH), bf16),
            pltpu.VMEM((slots, A, WIDTH), f32),
            pltpu.VMEM((slots, A, WIDTH), f32),
            pltpu.VMEM((slots, 2, 2 * LANES, 2 * LANES), bf16),
            pltpu.VMEM((slots, 2, LANES, 2 * LANES), bf16),
            pltpu.VMEM((slots, PAIRS, LANES), f32),
            pltpu.VMEM((PAIRS * CHUNK, 2 * LANES), f32),
            pltpu.VMEM((PAIRS * CHUNK, LANES), f32),
            pltpu.VMEM((n_store, n_queries), f32),
            pltpu.VMEM((n_store, n_queries), bf16),
            pltpu.VMEM((n_layer - 1, block, n_queries), bf16),
            pltpu.VMEM((n_queries, n_queries), bf16),
            dma((slots * n_chunks,)),
            dma,
            dma((slots, n_seq)),
            dma((slots, n_seq)),
            dma((n_seq,)),
            dma((slots, n_seq, n_chunks, HALVES)),
            dma((n_seq,)),
            dma((n_layer - 1,)),
            dma((n_layer - 1,)),
        ],
        compiler_params=pltpu.CompilerParams(
            collective_id=0, has_side_effects=True, vmem_limit_bytes=60 * 1024 * 1024
        ),
        name="gather_score",
    )(owner, store, queries, eig_in, eig_out, eig_val, query_order)


def solution(mesh):
    sizes = tuple(mesh.shape[axis] for axis in ("parts", "seq", "layer"))
    in_specs = (P(("parts", "seq"), "layer"), P("seq", "layer"), P(), P(), P(), P(), P())
    out_specs = P(("parts", "seq", "layer"), None)
    return jax.shard_map(
        functools.partial(on_device, sizes), mesh=mesh, in_specs=in_specs, out_specs=out_specs,
        check_vma=False,
    )
```

```python
import functools

import jax
import jax.numpy as jnp
from jax import lax
from jax.experimental import pallas as pl
from jax.experimental.pallas import tpu as pltpu
from jax.sharding import PartitionSpec as P

A = 32
B = 64
WIDTH = A * B
LANES = 2 * B
PAIRS = A // 2
CHUNK = 16
GROUP = 16
HALVES = 1
SPREAD = 2
MESH = pl.DeviceIdType.MESH
EXACT = lax.Precision.HIGHEST


def split(x):
    high = x.astype(jnp.bfloat16)
    return high, (x - high.astype(jnp.float32)).astype(jnp.bfloat16)


def kernel(
    sizes, owner_at, store, queries, eig_in_at, eig_out_at, eig_val_at, order_at, out,
    owner, eig_in, eig_out, eig_val, order, small_sem, raw, held, ready, mix_in, mix_back, both, small, inverse, wide, narrow, total, stage, sums, perm,
    raw_sem, held_sem, up_sem, down_sem, side_sem, arrive, side_arrive, part_sem, part_arrive,
):
    n_parts, n_seq, n_layer = sizes
    rows = queries.shape[0]
    n_chunks = rows // CHUNK
    block = out.shape[0]
    mine = lax.axis_index("parts")
    here = lax.axis_index("seq")
    layer = lax.axis_index("layer")
    other = 1 - mine

    barrier = pltpu.get_barrier_semaphore()

    def greet(**where):
        pl.semaphore_signal(barrier, inc=1, device_id=where, device_id_type=MESH)

    @pl.when(here > 0)
    def _():
        greet(seq=here - 1)

    @pl.when(here < n_seq - 1)
    def _():
        greet(seq=here + 1)

    greet(parts=other)
    for step in range(1, n_layer):
        greet(layer=lax.rem(layer + step, n_layer))

    def chunk_of(n):
        return jnp.where(n < n_chunks, n, 2 * n_chunks - 1 - n)

    def fetch(n):
        slot = jnp.where(n < n_chunks, mine, other)
        piece = (
            pl.ds(pl.multiple_of(chunk_of(n) * CHUNK, CHUNK), CHUNK),
            pl.ds(pl.multiple_of(slot * WIDTH, WIDTH), WIDTH),
        )
        return pltpu.make_async_copy(queries.at[piece], raw.at[n], raw_sem.at[n])

    tables = [
        pltpu.make_async_copy(source, target, small_sem.at[i])
        for i, (source, target) in enumerate((
            (owner_at, owner), (eig_in_at, eig_in), (eig_out_at, eig_out), (eig_val_at, eig_val),
            (order_at, order),
        ))
    ]
    for table in tables:
        table.start()
    fetch(0).start()
    fetch_store = pltpu.make_async_copy(store, held, held_sem)

    for table in tables:
        table.wait()
    for n in range(1, 2 * n_chunks):
        fetch(n).start()
    fetch_store.start()

    def setup(slot):
        model = owner[layer * 2 + slot]
        basis_in = eig_in[model]
        basis_out = eig_out[model]
        spread = (
            lax.shift_right_logical(lax.broadcasted_iota(jnp.int32, (A, WIDTH), 1), 6)
            == lax.broadcasted_iota(jnp.int32, (A, WIDTH), 0)
        ).astype(jnp.float32)
        mix_in[slot] = jnp.dot(basis_in, spread, precision=EXACT, preferred_element_type=jnp.float32)
        mix_back[slot] = lax.dot_general(
            basis_in, spread, (((0,), (0,)), ((), ())), precision=EXACT,
            preferred_element_type=jnp.float32,
        )
        twice = (
            lax.broadcasted_iota(jnp.int32, (B, LANES), 1) & (B - 1)
            == lax.broadcasted_iota(jnp.int32, (B, LANES), 0)
        ).astype(jnp.float32)
        both[slot] = jnp.zeros(both.shape[1:], both.dtype)
        small[slot] = jnp.zeros(small.shape[1:], small.dtype)
        for way, dims in enumerate((1, 0)):
            doubled = lax.dot_general(
                basis_out, twice, (((dims,), (0,)), ((), ())), precision=EXACT,
                preferred_element_type=jnp.float32,
            )
            high, low = split(doubled)
            for at in range(2):
                column = pl.ds(at * LANES, LANES)
                both[slot, way, pl.ds(at * B, B), column] = high
                both[slot, way, pl.ds(LANES + at * B, B), column] = high
                small[slot, way, pl.ds(at * B, B), column] = low
        values = jnp.dot(
            1.0 / (eig_val[model] + 0.1), twice, precision=EXACT, preferred_element_type=jnp.float32
        )
        pair = lax.broadcasted_iota(jnp.int32, (PAIRS, A), 0) * 2
        slots = lax.broadcasted_iota(jnp.int32, (PAIRS, A), 1)
        even = jnp.dot((slots == pair).astype(jnp.float32), values, precision=EXACT,
                       preferred_element_type=jnp.float32)
        odd = jnp.dot((slots == pair + 1).astype(jnp.float32), values, precision=EXACT,
                      preferred_element_type=jnp.float32)
        lane = lax.broadcasted_iota(jnp.int32, (PAIRS, LANES), 1)
        inverse[slot] = jnp.where(lane < B, even, odd)

    def rotate(x, slot, way):
        high, low = split(x)
        wide[...] = jnp.dot(
            jnp.concatenate([high, low], axis=1), both[slot, way], preferred_element_type=jnp.float32
        ) + jnp.dot(high, small[slot, way], preferred_element_type=jnp.float32)

    def mix(weights, slot, first):
        sums_of = [None] * GROUP
        for a in range(A):
            y = wide[pl.ds(CHUNK * (a // 2), CHUNK), pl.ds(LANES * (a % 2), LANES)]
            for g in range(GROUP):
                w = weights[slot, pl.ds(a, 1), pl.ds(pl.multiple_of((first + g) * LANES, LANES), LANES)]
                term = w * y
                sums_of[g] = term if a == 0 else sums_of[g] + term
        return sums_of

    def at_rows(source, k):
        return pl.ds(pl.multiple_of(source * rows + k * CHUNK, CHUNK), CHUNK)

    def precondition(slot, n, k):
        x = jnp.concatenate(
            [raw[n, :, pl.ds(c * LANES, LANES)] for c in range(PAIRS)], axis=0
        )
        rotate(x, slot, 0)

        def inner(i, _):
            for g, value in enumerate(mix(mix_in, slot, i * GROUP)):
                pair = i * GROUP + g
                narrow[pl.ds(pl.multiple_of(pair * CHUNK, CHUNK), CHUNK), :] = (
                    value * inverse[slot, pl.ds(pair, 1), :]
                )
            return 0

        lax.fori_loop(0, PAIRS // GROUP, inner, 0)
        rotate(narrow[...], slot, 1)

        def outer(i, _):
            for g, value in enumerate(mix(mix_back, slot, i * GROUP)):
                column = pl.ds(pl.multiple_of((i * GROUP + g) * LANES, LANES), LANES)
                ready[slot, at_rows(here, k), column] = value.astype(jnp.bfloat16)
            return 0

        lax.fori_loop(0, PAIRS // GROUP, outer, 0)

    def copy(piece, sem, arrival, **where):
        return pltpu.make_async_remote_copy(
            src_ref=piece, dst_ref=piece, send_sem=sem, recv_sem=arrival,
            device_id=where, device_id_type=MESH,
        )

    def halves(slot, source, k):
        for h in range(HALVES):
            yield (
                ready.at[slot, at_rows(source, k), pl.ds(h * (WIDTH // HALVES), WIDTH // HALVES)],
                arrive.at[slot, source, k, h],
            )

    def go_up(slot, source, piece, arrival):
        @pl.when(here < n_seq - 1)
        def _():
            copy(piece, up_sem.at[slot, source], arrival, seq=here + 1).start()

    def go_down(slot, source, piece, arrival):
        @pl.when(here > 0)
        def _():
            copy(piece, down_sem.at[slot, source], arrival, seq=here - 1).start()

    def pass_on(slot, source, k, is_end, ways):
        for piece, arrival in halves(slot, source, k):
            copy(piece, side_sem.at[source], arrival, parts=other).wait_recv()
            for way in ways:
                way(slot, source, piece, arrival)
            if slot is mine:
                @pl.when(jnp.logical_not(is_end & (k == n_chunks - 1)))
                def _():
                    copy(piece, side_sem.at[source], side_arrive.at[source], parts=other).start()

    def pass_all(n):
        distance, k = 1 + n // (n_chunks + 1), lax.rem(n, n_chunks + 1)
        below, above = here - distance, here + distance
        for source, exists, is_end, way in (
            (below, below >= 0, below == 0, go_up),
            (above, above < n_seq, above == n_seq - 1, go_down),
        ):
            @pl.when(exists & (k < n_chunks))
            def _():
                pass_on(mine, source, k, is_end, (way,))

            @pl.when(exists & (k == n_chunks) & is_end)
            def _():
                pass_on(other, source, n_chunks - 1, is_end, (way,))

    n_greetings = (
        jnp.where(here > 0, 1, 0) + jnp.where(here < n_seq - 1, 1, 0) + n_layer
    )

    def score(slot):
        return lax.dot_general(
            held[:, pl.ds(pl.multiple_of(slot * WIDTH, WIDTH), WIDTH)], ready[slot],
            (((1,), (1,)), ((), ())), preferred_element_type=jnp.float32,
        )

    n_passes = (n_seq - 1) * (n_chunks + 1)

    def job(n, _):
        slot = jnp.where(n < n_chunks, mine, other)
        late = n - n_chunks
        task = jnp.where(n < n_chunks, n, n_chunks + late // SPREAD)
        due = (n < n_chunks) | ((lax.rem(late, SPREAD) == 0) & (task < 2 * n_chunks))

        @pl.when(n == 1)
        def _():
            pl.semaphore_wait(barrier, n_greetings)

        @pl.when((n >= 1) & (n <= n_chunks))
        def _():
            for piece, arrival in halves(mine, here, n - 1):
                go_up(mine, here, piece, arrival)
                go_down(mine, here, piece, arrival)

        @pl.when((n == n_chunks + 1) & ((here == 0) | (here == n_seq - 1)))
        def _():
            for piece, arrival in halves(other, here, n_chunks - 1):
                go_up(other, here, piece, arrival)
                go_down(other, here, piece, arrival)

        @pl.when(n == n_chunks + n_passes - 1)
        def _():
            fetch_store.wait()
            total[...] = score(mine)

        @pl.when((n >= n_chunks) & (n < n_chunks + n_passes))
        def _():
            pass_all(n - n_chunks)

        @pl.when((n == 0) | (n == n_chunks))
        def _():
            setup(slot)

        @pl.when(due)
        def _():
            fetch(task).wait()
            precondition(slot, task, chunk_of(task))

        return 0

    n_steps = n_chunks + max(n_passes, SPREAD * n_chunks)
    lax.fori_loop(0, n_steps, job, 0)

    def slab(slot, source, size):
        return ready.at[slot, pl.ds(pl.multiple_of(source * rows, CHUNK), size), :]

    def each_source(do):
        def body(source, _):
            @pl.when(source != here)
            def _():
                is_end = (source == 0) | (source == n_seq - 1)

                @pl.when(jnp.logical_not(is_end))
                def _():
                    do(source, rows)

                if rows > CHUNK:
                    @pl.when(is_end)
                    def _():
                        do(source, rows - CHUNK)

            return 0

        lax.fori_loop(0, n_seq, body, 0)

    def side_slab(slot, source, size):
        return copy(slab(slot, source, size), side_sem.at[source], side_arrive.at[source], parts=other)

    each_source(lambda source, size: side_slab(other, source, size).wait_recv())
    total[...] += score(other)

    stage[...] = total[...].astype(jnp.bfloat16)

    def part(step):
        to = lax.rem(layer + step, n_layer)
        return pltpu.make_async_remote_copy(
            src_ref=stage.at[pl.ds(pl.multiple_of(to * block, CHUNK), block), :],
            dst_ref=sums.at[step - 1], send_sem=part_sem.at[step - 1],
            recv_sem=part_arrive.at[step - 1], device_id={"layer": to}, device_id_type=MESH,
        )

    for step in range(1, n_layer):
        part(step).start()

    which = lax.broadcasted_iota(jnp.int32, perm.shape, 0)
    perm[...] = (which == order[...].reshape(1, perm.shape[1])).astype(jnp.bfloat16)

    each_source(lambda source, size: side_slab(mine, source, size).wait_send())

    def drain(source, _):
        for comes, has_next, sems, where, is_end in (
            (source <= here, here < n_seq - 1, up_sem, here + 1, source == 0),
            (source >= here, here > 0, down_sem, here - 1, source == n_seq - 1),
        ):
            @pl.when(comes & has_next)
            def _():
                copy(slab(mine, source, rows), sems.at[mine, source], arrive.at[mine, source, 0, 0],
                     seq=where).wait_send()

            @pl.when(comes & has_next & is_end)
            def _():
                copy(slab(other, source, CHUNK), sems.at[other, source],
                     arrive.at[other, source, 0, 0], seq=where).wait_send()

        return 0

    lax.fori_loop(0, n_seq, drain, 0)

    result = total[pl.ds(pl.multiple_of(layer * block, CHUNK), block), :]
    for step in range(1, n_layer):
        part(step).wait_recv()
        result = result + sums[step - 1].astype(jnp.float32)
    high, low = split(result)
    out[...] = sum(
        jnp.dot(piece, perm[...], preferred_element_type=jnp.float32) for piece in (low, high)
    )
    for step in range(1, n_layer):
        part(step).wait_send()


def on_device(sizes, store, queries, owner, eig_in, eig_out, eig_val, query_order):
    n_parts, n_seq, n_layer = sizes
    rows = queries.shape[0]
    n_queries = rows * n_seq
    n_store = store.shape[0]
    n_chunks = rows // CHUNK
    slots = store.shape[1] // WIDTH
    assert slots == 2 and n_parts == 2 and rows % CHUNK == 0
    block = n_store // n_layer
    vmem = pl.BlockSpec(memory_space=pltpu.VMEM)
    anywhere = pl.BlockSpec(memory_space=pl.ANY)
    f32, bf16 = jnp.float32, jnp.bfloat16
    dma = pltpu.SemaphoreType.DMA
    return pl.pallas_call(
        functools.partial(kernel, sizes),
        out_shape=jax.ShapeDtypeStruct((block, n_queries), f32),
        in_specs=[anywhere] * 7,
        out_specs=vmem,
        scratch_shapes=[
            pltpu.SMEM(owner.shape, owner.dtype),
            pltpu.VMEM(eig_in.shape, f32),
            pltpu.VMEM(eig_out.shape, f32),
            pltpu.VMEM(eig_val.shape, f32),
            pltpu.VMEM(query_order.shape, query_order.dtype),
            dma((5,)),
            pltpu.VMEM((slots * n_chunks, CHUNK, WIDTH), f32),
            pltpu.VMEM(store.shape, bf16),
            pltpu.VMEM((slots, n_queries, WIDTH), bf16),
            pltpu.VMEM((slots, A, WIDTH), f32),
            pltpu.VMEM((slots, A, WIDTH), f32),
            pltpu.VMEM((slots, 2, 2 * LANES, 2 * LANES), bf16),
            pltpu.VMEM((slots, 2, LANES, 2 * LANES), bf16),
            pltpu.VMEM((slots, PAIRS, LANES), f32),
            pltpu.VMEM((PAIRS * CHUNK, 2 * LANES), f32),
            pltpu.VMEM((PAIRS * CHUNK, LANES), f32),
            pltpu.VMEM((n_store, n_queries), f32),
            pltpu.VMEM((n_store, n_queries), bf16),
            pltpu.VMEM((n_layer - 1, block, n_queries), bf16),
            pltpu.VMEM((n_queries, n_queries), bf16),
            dma((slots * n_chunks,)),
            dma,
            dma((slots, n_seq)),
            dma((slots, n_seq)),
            dma((n_seq,)),
            dma((slots, n_seq, n_chunks, HALVES)),
            dma((n_seq,)),
            dma((n_layer - 1,)),
            dma((n_layer - 1,)),
        ],
        compiler_params=pltpu.CompilerParams(
            collective_id=0, has_side_effects=True, vmem_limit_bytes=60 * 1024 * 1024
        ),
        name="gather_score",
    )(owner, store, queries, eig_in, eig_out, eig_val, query_order)


def solution(mesh):
    sizes = tuple(mesh.shape[axis] for axis in ("parts", "seq", "layer"))
    in_specs = (P(("parts", "seq"), "layer"), P("seq", "layer"), P(), P(), P(), P(), P())
    out_specs = P(("parts", "seq", "layer"), None)
    return jax.shard_map(
        functools.partial(on_device, sizes), mesh=mesh, in_specs=in_specs, out_specs=out_specs,
        check_vma=False,
    )
```

```python
import functools

import jax
import jax.numpy as jnp
from jax import lax
from jax.experimental import pallas as pl
from jax.experimental.pallas import tpu as pltpu
from jax.sharding import PartitionSpec as P

A = 32
B = 64
WIDTH = A * B
LANES = 2 * B
PAIRS = A // 2
CHUNK = 16
GROUP = 16
HALVES = 2
SPREAD = 2
MESH = pl.DeviceIdType.MESH
EXACT = lax.Precision.HIGHEST


def split(x):
    high = x.astype(jnp.bfloat16)
    return high, (x - high.astype(jnp.float32)).astype(jnp.bfloat16)


def kernel(
    sizes, owner_at, store, queries, eig_in_at, eig_out_at, eig_val_at, order_at, out,
    owner, eig_in, eig_out, eig_val, order, small_sem, raw, held, ready, mix_in, mix_back, both, small, inverse, wide, narrow, total, stage, sums, perm,
    raw_sem, held_sem, up_sem, down_sem, side_sem, arrive, side_arrive, part_sem, part_arrive,
):
    n_parts, n_seq, n_layer = sizes
    rows = queries.shape[0]
    n_chunks = rows // CHUNK
    block = out.shape[0]
    mine = lax.axis_index("parts")
    here = lax.axis_index("seq")
    layer = lax.axis_index("layer")
    other = 1 - mine

    barrier = pltpu.get_barrier_semaphore()

    def greet(**where):
        pl.semaphore_signal(barrier, inc=1, device_id=where, device_id_type=MESH)

    @pl.when(here > 0)
    def _():
        greet(seq=here - 1)

    @pl.when(here < n_seq - 1)
    def _():
        greet(seq=here + 1)

    greet(parts=other)
    for step in range(1, n_layer):
        greet(layer=lax.rem(layer + step, n_layer))

    def chunk_of(n):
        return jnp.where(n < n_chunks, n, 2 * n_chunks - 1 - n)

    def fetch(n):
        slot = jnp.where(n < n_chunks, mine, other)
        piece = (
            pl.ds(pl.multiple_of(chunk_of(n) * CHUNK, CHUNK), CHUNK),
            pl.ds(pl.multiple_of(slot * WIDTH, WIDTH), WIDTH),
        )
        return pltpu.make_async_copy(queries.at[piece], raw.at[n], raw_sem.at[n])

    tables = [
        pltpu.make_async_copy(source, target, small_sem.at[i])
        for i, (source, target) in enumerate((
            (owner_at, owner), (eig_in_at, eig_in), (eig_out_at, eig_out), (eig_val_at, eig_val),
            (order_at, order),
        ))
    ]
    for table in tables:
        table.start()
    fetch(0).start()
    fetch_store = pltpu.make_async_copy(store, held, held_sem)

    for table in tables:
        table.wait()
    for n in range(1, 2 * n_chunks):
        fetch(n).start()
    fetch_store.start()

    def setup(slot):
        model = owner[layer * 2 + slot]
        basis_in = eig_in[model]
        basis_out = eig_out[model]
        spread = (
            lax.shift_right_logical(lax.broadcasted_iota(jnp.int32, (A, WIDTH), 1), 6)
            == lax.broadcasted_iota(jnp.int32, (A, WIDTH), 0)
        ).astype(jnp.float32)
        mix_in[slot] = jnp.dot(basis_in, spread, precision=EXACT, preferred_element_type=jnp.float32)
        mix_back[slot] = lax.dot_general(
            basis_in, spread, (((0,), (0,)), ((), ())), precision=EXACT,
            preferred_element_type=jnp.float32,
        )
        twice = (
            lax.broadcasted_iota(jnp.int32, (B, LANES), 1) & (B - 1)
            == lax.broadcasted_iota(jnp.int32, (B, LANES), 0)
        ).astype(jnp.float32)
        both[slot] = jnp.zeros(both.shape[1:], both.dtype)
        small[slot] = jnp.zeros(small.shape[1:], small.dtype)
        for way, dims in enumerate((1, 0)):
            doubled = lax.dot_general(
                basis_out, twice, (((dims,), (0,)), ((), ())), precision=EXACT,
                preferred_element_type=jnp.float32,
            )
            high, low = split(doubled)
            for at in range(2):
                column = pl.ds(at * LANES, LANES)
                both[slot, way, pl.ds(at * B, B), column] = high
                both[slot, way, pl.ds(LANES + at * B, B), column] = high
                small[slot, way, pl.ds(at * B, B), column] = low
        values = jnp.dot(
            1.0 / (eig_val[model] + 0.1), twice, precision=EXACT, preferred_element_type=jnp.float32
        )
        pair = lax.broadcasted_iota(jnp.int32, (PAIRS, A), 0) * 2
        slots = lax.broadcasted_iota(jnp.int32, (PAIRS, A), 1)
        even = jnp.dot((slots == pair).astype(jnp.float32), values, precision=EXACT,
                       preferred_element_type=jnp.float32)
        odd = jnp.dot((slots == pair + 1).astype(jnp.float32), values, precision=EXACT,
                      preferred_element_type=jnp.float32)
        lane = lax.broadcasted_iota(jnp.int32, (PAIRS, LANES), 1)
        inverse[slot] = jnp.where(lane < B, even, odd)

    def rotate(x, slot, way):
        high, low = split(x)
        wide[...] = jnp.dot(
            jnp.concatenate([high, low], axis=1), both[slot, way], preferred_element_type=jnp.float32
        ) + jnp.dot(high, small[slot, way], preferred_element_type=jnp.float32)

    def mix(weights, slot, first):
        sums_of = [None] * GROUP
        for a in range(A):
            y = wide[pl.ds(CHUNK * (a // 2), CHUNK), pl.ds(LANES * (a % 2), LANES)]
            for g in range(GROUP):
                w = weights[slot, pl.ds(a, 1), pl.ds(pl.multiple_of((first + g) * LANES, LANES), LANES)]
                term = w * y
                sums_of[g] = term if a == 0 else sums_of[g] + term
        return sums_of

    def at_rows(source, k):
        return pl.ds(pl.multiple_of(source * rows + k * CHUNK, CHUNK), CHUNK)

    def precondition(slot, n, k):
        x = jnp.concatenate(
            [raw[n, :, pl.ds(c * LANES, LANES)] for c in range(PAIRS)], axis=0
        )
        rotate(x, slot, 0)

        def inner(i, _):
            for g, value in enumerate(mix(mix_in, slot, i * GROUP)):
                pair = i * GROUP + g
                narrow[pl.ds(pl.multiple_of(pair * CHUNK, CHUNK), CHUNK), :] = (
                    value * inverse[slot, pl.ds(pair, 1), :]
                )
            return 0

        lax.fori_loop(0, PAIRS // GROUP, inner, 0)
        rotate(narrow[...], slot, 1)

        def outer(i, _):
            for g, value in enumerate(mix(mix_back, slot, i * GROUP)):
                column = pl.ds(pl.multiple_of((i * GROUP + g) * LANES, LANES), LANES)
                ready[slot, at_rows(here, k), column] = value.astype(jnp.bfloat16)
            return 0

        lax.fori_loop(0, PAIRS // GROUP, outer, 0)

    def copy(piece, sem, arrival, **where):
        return pltpu.make_async_remote_copy(
            src_ref=piece, dst_ref=piece, send_sem=sem, recv_sem=arrival,
            device_id=where, device_id_type=MESH,
        )

    def halves(slot, source, k):
        for h in range(HALVES):
            yield (
                ready.at[slot, at_rows(source, k), pl.ds(h * (WIDTH // HALVES), WIDTH // HALVES)],
                arrive.at[slot, source, k, h],
            )

    def go_up(slot, source, piece, arrival):
        @pl.when(here < n_seq - 1)
        def _():
            copy(piece, up_sem.at[slot, source], arrival, seq=here + 1).start()

    def go_down(slot, source, piece, arrival):
        @pl.when(here > 0)
        def _():
            copy(piece, down_sem.at[slot, source], arrival, seq=here - 1).start()

    def pass_on(slot, source, k, is_end, ways):
        for piece, arrival in halves(slot, source, k):
            copy(piece, side_sem.at[source], arrival, parts=other).wait_recv()
            for way in ways:
                way(slot, source, piece, arrival)
            if slot is mine:
                @pl.when(jnp.logical_not(is_end & (k == n_chunks - 1)))
                def _():
                    copy(piece, side_sem.at[source], side_arrive.at[source], parts=other).start()

    def pass_all(n):
        distance, k = 1 + n // (n_chunks + 1), lax.rem(n, n_chunks + 1)
        below, above = here - distance, here + distance
        low = here < n_seq // 2
        for source, exists, is_end, way, when in (
            (above, above < n_seq, above == n_seq - 1, go_down, low),
            (below, below >= 0, below == 0, go_up, True),
            (above, above < n_seq, above == n_seq - 1, go_down, jnp.logical_not(low)),
        ):
            exists = exists & when
            @pl.when(exists & (k < n_chunks))
            def _():
                pass_on(mine, source, k, is_end, (way,))

            @pl.when(exists & (k == n_chunks) & is_end)
            def _():
                pass_on(other, source, n_chunks - 1, is_end, (way,))

    n_greetings = (
        jnp.where(here > 0, 1, 0) + jnp.where(here < n_seq - 1, 1, 0) + n_layer
    )

    def score(slot):
        return lax.dot_general(
            held[:, pl.ds(pl.multiple_of(slot * WIDTH, WIDTH), WIDTH)], ready[slot],
            (((1,), (1,)), ((), ())), preferred_element_type=jnp.float32,
        )

    n_passes = (n_seq - 1) * (n_chunks + 1)

    def job(n, _):
        slot = jnp.where(n < n_chunks, mine, other)
        late = n - n_chunks
        task = jnp.where(n < n_chunks, n, n_chunks + late // SPREAD)
        due = (n < n_chunks) | ((lax.rem(late, SPREAD) == 0) & (task < 2 * n_chunks))

        @pl.when(n == 1)
        def _():
            pl.semaphore_wait(barrier, n_greetings)

        @pl.when((n >= 1) & (n <= n_chunks))
        def _():
            for piece, arrival in halves(mine, here, n - 1):
                go_up(mine, here, piece, arrival)
                go_down(mine, here, piece, arrival)

        @pl.when((n == n_chunks + 1) & ((here == 0) | (here == n_seq - 1)))
        def _():
            for piece, arrival in halves(other, here, n_chunks - 1):
                go_up(other, here, piece, arrival)
                go_down(other, here, piece, arrival)

        @pl.when(n == n_chunks + n_passes - 1)
        def _():
            fetch_store.wait()
            total[...] = score(mine)

        @pl.when((n >= n_chunks) & (n < n_chunks + n_passes))
        def _():
            pass_all(n - n_chunks)

        @pl.when((n == 0) | (n == n_chunks))
        def _():
            setup(slot)

        @pl.when(due)
        def _():
            fetch(task).wait()
            precondition(slot, task, chunk_of(task))

        return 0

    n_steps = n_chunks + max(n_passes, SPREAD * n_chunks)
    lax.fori_loop(0, n_steps, job, 0)

    def slab(slot, source, size):
        return ready.at[slot, pl.ds(pl.multiple_of(source * rows, CHUNK), size), :]

    def each_source(do):
        def body(source, _):
            @pl.when(source != here)
            def _():
                is_end = (source == 0) | (source == n_seq - 1)

                @pl.when(jnp.logical_not(is_end))
                def _():
                    do(source, rows)

                if rows > CHUNK:
                    @pl.when(is_end)
                    def _():
                        do(source, rows - CHUNK)

            return 0

        lax.fori_loop(0, n_seq, body, 0)

    def side_slab(slot, source, size):
        return copy(slab(slot, source, size), side_sem.at[source], side_arrive.at[source], parts=other)

    each_source(lambda source, size: side_slab(other, source, size).wait_recv())
    total[...] += score(other)

    stage[...] = total[...].astype(jnp.bfloat16)

    def part(step):
        to = lax.rem(layer + step, n_layer)
        return pltpu.make_async_remote_copy(
            src_ref=stage.at[pl.ds(pl.multiple_of(to * block, CHUNK), block), :],
            dst_ref=sums.at[step - 1], send_sem=part_sem.at[step - 1],
            recv_sem=part_arrive.at[step - 1], device_id={"layer": to}, device_id_type=MESH,
        )

    for step in (*range(2, n_layer), 1):
        part(step).start()

    which = lax.broadcasted_iota(jnp.int32, perm.shape, 0)
    perm[...] = (which == order[...].reshape(1, perm.shape[1])).astype(jnp.bfloat16)

    each_source(lambda source, size: side_slab(mine, source, size).wait_send())

    def drain(source, _):
        for comes, has_next, sems, where, is_end in (
            (source <= here, here < n_seq - 1, up_sem, here + 1, source == 0),
            (source >= here, here > 0, down_sem, here - 1, source == n_seq - 1),
        ):
            @pl.when(comes & has_next)
            def _():
                copy(slab(mine, source, rows), sems.at[mine, source], arrive.at[mine, source, 0, 0],
                     seq=where).wait_send()

            @pl.when(comes & has_next & is_end)
            def _():
                copy(slab(other, source, CHUNK), sems.at[other, source],
                     arrive.at[other, source, 0, 0], seq=where).wait_send()

        return 0

    lax.fori_loop(0, n_seq, drain, 0)

    result = total[pl.ds(pl.multiple_of(layer * block, CHUNK), block), :]
    for step in range(1, n_layer):
        part(step).wait_recv()
        result = result + sums[step - 1].astype(jnp.float32)
    high, low = split(result)
    out[...] = sum(
        jnp.dot(piece, perm[...], preferred_element_type=jnp.float32) for piece in (low, high)
    )
    for step in range(1, n_layer):
        part(step).wait_send()


def on_device(sizes, store, queries, owner, eig_in, eig_out, eig_val, query_order):
    n_parts, n_seq, n_layer = sizes
    rows = queries.shape[0]
    n_queries = rows * n_seq
    n_store = store.shape[0]
    n_chunks = rows // CHUNK
    slots = store.shape[1] // WIDTH
    assert slots == 2 and n_parts == 2 and rows % CHUNK == 0
    block = n_store // n_layer
    vmem = pl.BlockSpec(memory_space=pltpu.VMEM)
    anywhere = pl.BlockSpec(memory_space=pl.ANY)
    f32, bf16 = jnp.float32, jnp.bfloat16
    dma = pltpu.SemaphoreType.DMA
    return pl.pallas_call(
        functools.partial(kernel, sizes),
        out_shape=jax.ShapeDtypeStruct((block, n_queries), f32),
        in_specs=[anywhere] * 7,
        out_specs=vmem,
        scratch_shapes=[
            pltpu.SMEM(owner.shape, owner.dtype),
            pltpu.VMEM(eig_in.shape, f32),
            pltpu.VMEM(eig_out.shape, f32),
            pltpu.VMEM(eig_val.shape, f32),
            pltpu.VMEM(query_order.shape, query_order.dtype),
            dma((5,)),
            pltpu.VMEM((slots * n_chunks, CHUNK, WIDTH), f32),
            pltpu.VMEM(store.shape, bf16),
            pltpu.VMEM((slots, n_queries, WIDTH), bf16),
            pltpu.VMEM((slots, A, WIDTH), f32),
            pltpu.VMEM((slots, A, WIDTH), f32),
            pltpu.VMEM((slots, 2, 2 * LANES, 2 * LANES), bf16),
            pltpu.VMEM((slots, 2, LANES, 2 * LANES), bf16),
            pltpu.VMEM((slots, PAIRS, LANES), f32),
            pltpu.VMEM((PAIRS * CHUNK, 2 * LANES), f32),
            pltpu.VMEM((PAIRS * CHUNK, LANES), f32),
            pltpu.VMEM((n_store, n_queries), f32),
            pltpu.VMEM((n_store, n_queries), bf16),
            pltpu.VMEM((n_layer - 1, block, n_queries), bf16),
            pltpu.VMEM((n_queries, n_queries), bf16),
            dma((slots * n_chunks,)),
            dma,
            dma((slots, n_seq)),
            dma((slots, n_seq)),
            dma((n_seq,)),
            dma((slots, n_seq, n_chunks, HALVES)),
            dma((n_seq,)),
            dma((n_layer - 1,)),
            dma((n_layer - 1,)),
        ],
        compiler_params=pltpu.CompilerParams(
            collective_id=0, has_side_effects=True, vmem_limit_bytes=60 * 1024 * 1024
        ),
        name="gather_score",
    )(owner, store, queries, eig_in, eig_out, eig_val, query_order)


def solution(mesh):
    sizes = tuple(mesh.shape[axis] for axis in ("parts", "seq", "layer"))
    in_specs = (P(("parts", "seq"), "layer"), P("seq", "layer"), P(), P(), P(), P(), P())
    out_specs = P(("parts", "seq", "layer"), None)
    return jax.shard_map(
        functools.partial(on_device, sizes), mesh=mesh, in_specs=in_specs, out_specs=out_specs,
        check_vma=False,
    )
```
